32 devices in a mesh: lat: 8 (over y, x, core), lon: 4 (over z).
Axes of the slice: x: 2, y: 2, z: 4, core: 2. Of those that a mesh axis runs over, the one named last changes fastest.
Arguments:
- state: float32 [256, 128, 512], P(None, 'lat', 'lon'), may hold values from -6 to 6
- north_coef: float32 [128, 512], P('lat', 'lon'), may hold values from 0.03 to 0.24
- east_coef: float32 [128, 512], P('lat', 'lon'), may hold values from 0.03 to 0.24
- land_mask: int32 [128, 512], P('lat', 'lon'), may hold values 0 or 1
- owner_slot: int32 [128, 512], P('lat', 'lon'), may hold values from 0 to 65535, as said below
- w_in: bfloat16 [512, 256], replicated, may hold values from -0.375 to 0.375
- w_mid: bfloat16 [512, 512], replicated, may hold values from -0.25 to 0.25
- w_out: bfloat16 [256, 512], replicated, may hold values from -0.25 to 0.25
- w_land: float32 [512], replicated, may hold values from -4 to 4
- tend_cot: bfloat16 [256, 65536], P(None, ('lat', 'lon')), may hold values from -6 to 6
Outputs:
- new_state: float32 [256, 128, 512], P(None, 'lat', 'lon')
- grad_in: float32 [512, 256], replicated
- grad_mid: float32 [512, 512], replicated
- grad_out: float32 [256, 512], replicated
- grad_land: float32 [512], replicated
The draws below stay inside these ranges and needn't reach their ends.
Inputs may be any that keep to these rules, and one draw needn't show every extreme that they name: owner_slot holds each of its values once. Owner slot // 2048 counts devices along lat then lon, as tend_cot's columns are laid out. For a column in the 16 x 128 tile of device s (counted the same way), slot % 2048 // 64 equals s, so each device has exactly 64 columns for each owner.
All inputs are finite; a program needn't handle non-finite values. No bound on the sum of `land_mask` on one device may be relied on, other than what follows from the above.
Results may differ from the reference program's by a relative error of at most 0.0054.
Values may be sent and summed in bfloat16 or wider, within the bound.
A program may use at most 128 MiB of HBM per device.

```python
import math
import jax
import jax.numpy as jnp
from jax import lax

FIELDS = 8
LEVELS = 32
HIDDEN_SIZE = 512
SUBSTEPS = 3
TLAT = 16
TLON = 128
CHANS = 256
NLAT = 128
NLON = 512
COL_DEV = 2048
NCOL = 65536
SENDS = 64
N_LAT = 8
N_LON = 4


def draw_owner_slot(key, part):
    key = jax.random.fold_in(key, 7)
    device_count = N_LAT * N_LON
    keys = jax.random.split(key, device_count)
    orders = jax.vmap(lambda one: jax.random.permutation(one, COL_DEV))(keys).astype(jnp.int32)
    source = jnp.arange(device_count, dtype=jnp.int32)[:, None]
    slots = orders // SENDS * COL_DEV + source * SENDS + orders % SENDS
    slots = slots.reshape(N_LAT, N_LON, TLAT, TLON).transpose(0, 2, 1, 3).reshape(NLAT, NLON)
    return slots.astype(jnp.int32)


def plant(result, own_key, low, high):
    longest = result.shape.index(max(result.shape))
    spots = []
    for shift in (0, 1):
        where = [jax.random.randint(jax.random.fold_in(own_key, axis), (), 0, length) for axis, length in enumerate(result.shape)]
        where[longest] = (where[longest] + shift) % result.shape[longest]
        spots.append(tuple(where))
    return result.at[spots[0]].set(low).at[spots[1]].set(high)


def shard_levels(stream_key, dims, cuts, low, largest):
    def one(position, parts):
        steps = jax.random.uniform(jax.random.fold_in(jax.random.fold_in(stream_key, 6), position), (parts,), jnp.float32, low / len(cuts), largest / len(cuts))
        return jnp.repeat(jnp.exp(steps), dims[position] // parts).reshape((-1,) + (1,) * (len(dims) - position - 1))

    loudness = one(*cuts[0])
    for cut in cuts[1:]:
        loudness = loudness * one(*cut)
    return loudness


def noise(rng, shape, width, limit, pieces=(), kind=jnp.bfloat16):
    drawn = width * jax.random.normal(rng, shape, jnp.float32)
    if pieces:
        drawn = drawn * shard_levels(rng, shape, pieces, -0.22, 0.18)
    return jnp.clip(drawn, -limit, limit).astype(kind)


def setup_inputs(seed: int = 0) -> dict:
    streams_of = jax.random.split(jax.random.key(seed), 11)
    return {
        "state": noise(streams_of[0], (CHANS, NLAT, NLON), 1.0, 6.0, ((1, 8), (2, 4)), jnp.float32),
        "north_coef": jnp.clip(jnp.exp(math.log(0.24) - 2.0794415 * jax.random.uniform(streams_of[1], (NLAT, NLON), jnp.float32) ** shard_levels(streams_of[1], (NLAT, NLON), ((0, 8), (1, 4)), -0.2, 0.2)), 0.03, 0.24),
        "east_coef": jnp.clip(jnp.exp(math.log(0.24) - 2.0794415 * jax.random.uniform(streams_of[2], (NLAT, NLON), jnp.float32) ** shard_levels(streams_of[2], (NLAT, NLON), ((0, 8), (1, 4)), -0.2, 0.2)), 0.03, 0.24),
        "land_mask": plant((jax.random.randint(streams_of[3], (NLAT, NLON), 0, 10) < 3).astype(jnp.int32), jax.random.fold_in(streams_of[3], 1), 0, 1),
        "owner_slot": draw_owner_slot(jax.random.fold_in(streams_of[10], 71), 0),
        "w_in": noise(streams_of[5], (HIDDEN_SIZE, CHANS), CHANS ** -0.5, 0.375),
        "w_mid": noise(streams_of[6], (HIDDEN_SIZE, HIDDEN_SIZE), HIDDEN_SIZE ** -0.5, 0.25),
        "w_out": noise(streams_of[7], (CHANS, HIDDEN_SIZE), HIDDEN_SIZE ** -0.5, 0.25),
        "w_land": noise(streams_of[8], (HIDDEN_SIZE,), 1.0, 4.0, (), jnp.float32),
        "tend_cot": noise(streams_of[9], (CHANS, NCOL), 1.0, 6.0, ((1, 32),)),
    }


def substep(field, north_face, east_coef):
    flux_north = north_face[None] * (jnp.roll(field, -1, 1) - field)
    flux_east = east_coef[None] * (jnp.roll(field, -1, 2) - field)
    return field + flux_north - jnp.roll(flux_north, 1, 1) + flux_east - jnp.roll(flux_east, 1, 2)


def physics(feeds, land, cot_cols, w_in, w_mid, w_out, w_land):
    pre_first = jnp.dot(w_in, feeds, preferred_element_type=jnp.float32) + w_land[:, None] * land.astype(jnp.float32)[None, :]
    sig_first = jax.nn.sigmoid(pre_first)
    act_first = (pre_first * sig_first).astype(jnp.bfloat16)
    pre_second = jnp.dot(w_mid, act_first, preferred_element_type=jnp.float32)
    sig_second = jax.nn.sigmoid(pre_second)
    act_second = (pre_second * sig_second).astype(jnp.bfloat16)
    tendency = jnp.dot(w_out, act_second, preferred_element_type=jnp.float32).astype(jnp.bfloat16)
    grad_out = jnp.dot(cot_cols, act_second.T, preferred_element_type=jnp.float32)
    back_second = (jnp.dot(w_out.T, cot_cols, preferred_element_type=jnp.float32) * sig_second * (1.0 + pre_second * (1.0 - sig_second))).astype(jnp.bfloat16)
    grad_mid = jnp.dot(back_second, act_first.T, preferred_element_type=jnp.float32)
    back_first = (jnp.dot(w_mid.T, back_second, preferred_element_type=jnp.float32) * sig_first * (1.0 + pre_first * (1.0 - sig_first))).astype(jnp.bfloat16)
    grad_in = jnp.dot(back_first, feeds.T, preferred_element_type=jnp.float32)
    grad_land = jnp.dot(back_first, land, preferred_element_type=jnp.float32)
    return tendency, (grad_in, grad_mid, grad_out, grad_land)


def reference(state, north_coef, east_coef, land_mask, owner_slot, w_in, w_mid, w_out, w_land, tend_cot):
    row_index = jnp.arange(NLAT, dtype=jnp.int32)[:, None]
    north_face = jnp.where(row_index < NLAT - 1, north_coef, jnp.float32(0.0))

    def dycore(field):
        for step in range(SUBSTEPS):
            field = substep(field, north_face, east_coef)
        return field

    dynamic = lax.map(dycore, state.reshape(FIELDS, LEVELS, NLAT, NLON)).reshape(CHANS, NCOL)
    land_all = land_mask.reshape(NCOL).astype(jnp.bfloat16)
    cot_grid = jnp.take(tend_cot, owner_slot.reshape(NCOL), axis=1)
    blocks = NCOL // COL_DEV

    def one_block(totals, index):
        start = (index * COL_DEV).astype(jnp.int32)
        feeds = lax.dynamic_slice_in_dim(dynamic, start, COL_DEV, 1).astype(jnp.bfloat16)
        land = lax.dynamic_slice_in_dim(land_all, start, COL_DEV, 0)
        cot_cols = lax.dynamic_slice_in_dim(cot_grid, start, COL_DEV, 1)
        tendency, terms = physics(feeds, land, cot_cols, w_in, w_mid, w_out, w_land)
        return jax.tree.map(lambda a, b: a + b, totals, terms), tendency

    zeros = (jnp.zeros((HIDDEN_SIZE, CHANS), jnp.float32), jnp.zeros((HIDDEN_SIZE, HIDDEN_SIZE), jnp.float32), jnp.zeros((CHANS, HIDDEN_SIZE), jnp.float32), jnp.zeros((HIDDEN_SIZE,), jnp.float32))
    totals, tendencies = lax.scan(one_block, zeros, jnp.arange(blocks, dtype=jnp.int32))
    tendency = jnp.transpose(tendencies, (1, 0, 2)).reshape(CHANS, NCOL)
    new_state = (dynamic + tendency.astype(jnp.float32)).reshape(CHANS, NLAT, NLON)
    scale = jnp.float32(NCOL ** -0.5)
    return new_state, totals[0] * scale, totals[1] * scale, totals[2] * scale, totals[3] * scale
```

```python
import jax
import jax.numpy as jnp
from jax import lax
from jax.sharding import PartitionSpec as P

SUBSTEPS = 3


def padded_2(array, sides, width, wrap):
    for axis, dim in sides:
        size, length = (lax.axis_size(axis), array.shape[dim])
        up = [(i, (i + 1) % size) for i in range(size if wrap else size - 1)]
        down = [(j, i) for i, j in up]
        last = lax.slice_in_dim(array, length - width, length, axis=dim)
        leading = lax.slice_in_dim(array, 0, width, axis=dim)
        before = lax.ppermute(last, axis, up)
        after = lax.ppermute(leading, axis, down)
        array = jnp.concatenate([before, array, after], axis=dim)
    return array


def advance(padded, north_face, east_face):
    flux_north = north_face[None, :-1, :] * (padded[:, 1:, :] - padded[:, :-1, :])
    flux_east = east_face[None, :, :-1] * (padded[:, :, 1:] - padded[:, :, :-1])
    inner = padded[:, 1:-1, 1:-1]
    return (
        inner
        + flux_north[:, 1:, 1:-1]
        - flux_north[:, :-1, 1:-1]
        + flux_east[:, 1:-1, 1:]
        - flux_east[:, 1:-1, :-1]
    )


def physics(feeds, land, cot_cols, w_in, w_mid, w_out, w_land):
    pre_first = (
        jnp.dot(w_in, feeds, preferred_element_type=jnp.float32)
        + w_land[:, None] * land.astype(jnp.float32)[None, :]
    )
    sig_first = jax.nn.sigmoid(pre_first)
    act_first = (pre_first * sig_first).astype(jnp.bfloat16)
    pre_second = jnp.dot(w_mid, act_first, preferred_element_type=jnp.float32)
    sig_second = jax.nn.sigmoid(pre_second)
    act_second = (pre_second * sig_second).astype(jnp.bfloat16)
    tendency = jnp.dot(w_out, act_second, preferred_element_type=jnp.float32).astype(jnp.bfloat16)
    grad_out = jnp.dot(cot_cols, act_second.T, preferred_element_type=jnp.float32)
    back_second = (
        jnp.dot(w_out.T, cot_cols, preferred_element_type=jnp.float32)
        * sig_second
        * (1.0 + pre_second * (1.0 - sig_second))
    ).astype(jnp.bfloat16)
    grad_mid = jnp.dot(back_second, act_first.T, preferred_element_type=jnp.float32)
    back_first = (
        jnp.dot(w_mid.T, back_second, preferred_element_type=jnp.float32)
        * sig_first
        * (1.0 + pre_first * (1.0 - sig_first))
    ).astype(jnp.bfloat16)
    grad_in = jnp.dot(back_first, feeds.T, preferred_element_type=jnp.float32)
    grad_land = jnp.dot(back_first, land, preferred_element_type=jnp.float32)
    return (tendency, (grad_in, grad_mid, grad_out, grad_land))


def per_device(
    state, north_coef, east_coef, land_mask, owner_slot, w_in, w_mid, w_out, w_land, tend_cot
):
    channels, tile_rows, tile_cols = state.shape
    lat_count = lax.axis_size("lat")
    dev_count = lat_count * lax.axis_size("lon")
    columns = tile_rows * tile_cols
    per_owner = columns // dev_count
    cot_rows = tend_cot.T.reshape(dev_count, per_owner, channels)
    cot_rows = lax.all_to_all(cot_rows, ("lat", "lon"), split_axis=0, concat_axis=0, tiled=True)
    cot_rows = cot_rows.reshape(columns, channels)
    row_index = lax.axis_index("lat") * tile_rows + jnp.arange(tile_rows, dtype=jnp.int32)
    north_face = jnp.where(
        row_index[:, None] < tile_rows * lat_count - 1, north_coef, jnp.float32(0.0)
    )
    coefs = jnp.stack([north_face, east_coef])
    joined = jnp.concatenate([state, coefs], 0)
    joined = padded_2(joined, (("lat", 1),), SUBSTEPS, False)
    joined = padded_2(joined, (("lon", 2),), SUBSTEPS, True)
    field = joined[:channels]
    north, east = joined[channels], joined[channels + 1]
    for step in range(SUBSTEPS):
        field = advance(field, north, east)
        north, east = north[1:-1, 1:-1], east[1:-1, 1:-1]
    dynamic = field.reshape(channels, columns)
    slots = owner_slot.reshape(columns)
    place = slots // columns * per_owner + slots % per_owner
    pick = (jnp.arange(columns, dtype=jnp.int32)[:, None] == place[None, :]).astype(jnp.bfloat16)
    land = land_mask.reshape(columns).astype(jnp.bfloat16)
    cot_grid = lax.dot_general(
        cot_rows, pick, (((0,), (0,)), ((), ())), preferred_element_type=jnp.float32
    ).astype(jnp.bfloat16)
    tendency, gradients = physics(
        dynamic.astype(jnp.bfloat16), land, cot_grid, w_in, w_mid, w_out, w_land
    )
    new_state = (dynamic + tendency.astype(jnp.float32)).reshape(channels, tile_rows, tile_cols)
    scale = jnp.float32((columns * dev_count) ** (-0.5))
    summed = lax.psum(gradients, ("lat", "lon"))
    return (new_state,) + tuple(g * scale for g in summed)


def solution(mesh):
    placed = (
        P(None, "lat", "lon"),
        P("lat", "lon"),
        P("lat", "lon"),
        P("lat", "lon"),
        P("lat", "lon"),
        P(),
        P(),
        P(),
        P(),
        P(None, ("lat", "lon")),
    )
    return jax.shard_map(
        per_device,
        mesh=mesh,
        in_specs=placed,
        out_specs=(P(None, "lat", "lon"), P(), P(), P(), P()),
        check_vma=False,
    )
```

```python
import functools

import jax
import jax.numpy as jnp
from jax import lax
from jax.experimental import pallas as pl
from jax.experimental.pallas import tpu as pltpu
from jax.sharding import PartitionSpec as P

SUBSTEPS = 3
PAD = 16
F32 = jnp.float32
BF16 = jnp.bfloat16


def iota(shape, dim):
    return lax.broadcasted_iota(jnp.int32, shape, dim)


def dot(a, b):
    return jnp.dot(a, b, preferred_element_type=F32)


def dot_nt(a, b):
    return lax.dot_general(a, b, (((1,), (1,)), ((), ())), preferred_element_type=F32)


def kernel(
    n_lat,
    n_lon,
    state,
    north,
    east,
    land,
    place,
    w_in,
    w_mid,
    w_out,
    w_land,
    cot,
    new_state,
    grads,
    grad_land,
    ext,
    cn_ext,
    ce_ext,
    edge_rows,
    packed,
    halo_rx,
    pack_rx,
    strip_w,
    strip_e,
    cot_tx,
    cot_rx,
    cot_pl,
    pick,
    feeds,
    act1,
    act2,
    der1,
    der2,
    wt_out,
    wt_mid,
    part,
    land_acc,
    sum0,
    sum1,
    rx0,
    rx1,
    rx2,
    tx0,
    tx1,
    tx2,
    state_sem,
    out_sem,
    halo_send,
    halo_recv,
    a2a_send,
    a2a_recv,
    red_send,
    red_recv,
    gat_send,
    gat_recv,
):
    channels, rows, cols = state.shape
    devs = n_lat * n_lon
    columns = rows * cols
    block = columns // devs
    lat, lon = lax.axis_index("lat"), lax.axis_index("lon")
    me = lat * n_lon + lon

    def place_of(d):
        return (d // n_lon, lax.rem(d, n_lon))

    loads = [
        pltpu.make_async_copy(state.at[:, r, :], ext.at[r + 3], state_sem.at[r])
        for r in range(rows)
    ]
    for copy in loads:
        copy.start()

    barrier = pltpu.get_barrier_semaphore()

    @pl.loop(1, devs)
    def _(k):
        pl.semaphore_signal(
            barrier,
            inc=1,
            device_id=place_of(lax.rem(me + k, devs)),
            device_id_type=pl.DeviceIdType.MESH,
        )

    n_all, e_all = north[...], east[...]
    n_hi, e_hi = n_all.astype(BF16).astype(F32), e_all.astype(BF16).astype(F32)
    n_lo, e_lo = n_all - n_hi, e_all - e_hi
    sub = iota((PAD, cols), 0)
    kk, ll = iota((cols, cols), 0), iota((cols, cols), 1)
    spot = jnp.where(kk < 3, kk, jnp.where(kk >= cols - 3, kk - (cols - 6), -1000))
    cn_ext[3 : 3 + rows] = n_all
    ce_ext[3 : 3 + rows] = e_all
    total = jnp.zeros((channels + PAD, cols), F32)
    for r in range(rows):
        loads[r].wait()
        coef = jnp.where(
            sub == 0,
            n_hi[r : r + 1],
            jnp.where(
                sub == 1,
                n_lo[r : r + 1],
                jnp.where(sub == 2, e_hi[r : r + 1], jnp.where(sub == 3, e_lo[r : r + 1], 0.0)),
            ),
        )
        tile = jnp.concatenate([ext[r + 3].astype(BF16), coef.astype(BF16)], 0)
        if r < 3:
            edge_rows[0, r] = tile
        if r >= rows - 3:
            edge_rows[1, r - (rows - 3)] = tile
        total += dot(tile, (ll == spot + 6 * r).astype(BF16))
    packed[...] = total.astype(BF16)

    pl.semaphore_wait(barrier, devs - 1)
    up, down = lax.rem(lat + 1, n_lat), lax.rem(lat + n_lat - 1, n_lat)
    right, left = lax.rem(lon + 1, n_lon), lax.rem(lon + n_lon - 1, n_lon)
    sends = [
        (edge_rows.at[1], halo_rx.at[0], (up, lon)),
        (edge_rows.at[0], halo_rx.at[1], (down, lon)),
        (packed, pack_rx.at[0], (lat, right)),
        (packed, pack_rx.at[1], (lat, left)),
        (packed, pack_rx.at[2], (up, right)),
        (packed, pack_rx.at[3], (down, right)),
        (packed, pack_rx.at[4], (up, left)),
        (packed, pack_rx.at[5], (down, left)),
    ]
    halos = [
        pltpu.make_async_remote_copy(
            src_ref=src,
            dst_ref=dst,
            send_sem=halo_send.at[i],
            recv_sem=halo_recv.at[i],
            device_id=where,
            device_id_type=pl.DeviceIdType.MESH,
        )
        for i, (src, dst, where) in enumerate(sends)
    ]
    for copy in halos:
        copy.start()

    for j in range(columns // 128):
        cot_tx[j * 128 : (j + 1) * 128] = cot[:, j * 128 : (j + 1) * 128].T

    def exchange(k):
        there = lax.rem(me + k, devs)
        return pltpu.make_async_remote_copy(
            src_ref=cot_tx.at[pl.ds(pl.multiple_of(there * block, block), block)],
            dst_ref=cot_rx.at[pl.ds(pl.multiple_of(me * block, block), block)],
            send_sem=a2a_send.at[k],
            recv_sem=a2a_recv.at[me],
            device_id=place_of(there),
            device_id_type=pl.DeviceIdType.MESH,
        )

    def arrival(k):
        source = lax.rem(me + k, devs)
        return pltpu.make_async_remote_copy(
            src_ref=cot_tx.at[pl.ds(0, block)],
            dst_ref=cot_rx.at[pl.ds(pl.multiple_of(source * block, block), block)],
            send_sem=a2a_send.at[k],
            recv_sem=a2a_recv.at[source],
            device_id=place_of(source),
            device_id_type=pl.DeviceIdType.MESH,
        )

    @pl.loop(1, devs)
    def _(k):
        exchange(k).start()

    own = pl.ds(pl.multiple_of(me * block, block), block)
    cot_rx[own] = cot_tx[own]
    wt_out[...] = w_out[...].T
    wt_mid[...] = w_mid[...].T

    for copy in halos:
        copy.wait()
    for side, first in ((0, 0), (1, rows + 3)):
        for j in range(3):
            tile = halo_rx[side, j].astype(F32)
            ext[first + j] = tile[:channels]
            cn_ext[first + j : first + j + 1] = tile[channels : channels + 1] + tile[channels + 1 : channels + 2]
            ce_ext[first + j : first + j + 1] = tile[channels + 2 : channels + 3] + tile[channels + 3 : channels + 4]

    rest = kk - 6 * ((kk * 43) >> 8)
    low = (rest < 3) & (kk < 6 * rows)
    high = (rest >= 3) & (kk < 6 * rows)
    top, bottom = kk >= 6 * (rows - 2), kk < 12
    far = 6 * (rows + 2)

    def chosen(mask, offset):
        return (mask & (ll == kk + offset)).astype(BF16)

    last = 6 * (rows - 2)
    outer = [(halo_rx[0, 1], 0), (halo_rx[0, 2], 6), (halo_rx[1, 0], far), (halo_rx[1, 1], far + 6)]
    west = dot(packed[...], chosen(low, 15)) + dot(pack_rx[0], chosen(high, 9))
    west += dot(pack_rx[2], chosen(high & top, -last - 3)) + dot(pack_rx[3], chosen(high & bottom, far - 3))
    for tile, base in outer:
        west += dot(tile, chosen(kk < 3, base + 3))
    strip_w[...] = west
    right_side = dot(packed[...], chosen(high, 9)) + dot(pack_rx[1], chosen(low, 15))
    right_side += dot(pack_rx[4], chosen(low & top, 3 - last)) + dot(pack_rx[5], chosen(low & bottom, far + 3))
    for tile, base in outer:
        right_side += dot(tile, chosen(kk >= cols - 3, base - (cols - 3)))
    strip_e[...] = right_side

    chunk = 64
    lane = iota((chunk, cols), 1)

    def turn(x, by):
        return pltpu.roll(x, by % cols, 1)

    @pl.loop(0, channels // chunk)
    def _(c):
        here = pl.ds(pl.multiple_of(c * chunk, chunk), chunk)
        strips = []
        for ref in (strip_w, strip_e):
            cn = ref[channels : channels + 1] + ref[channels + 1 : channels + 2]
            ce = ref[channels + 2 : channels + 3] + ref[channels + 3 : channels + 4]
            strips.append([ref[here], cn, ce])
        for step in range(SUBSTEPS):
            fluxes = []
            for strip in strips:
                f, cn, ce = strip
                fluxes.append(ce * (turn(f, -1) - f))
            west_flux, east_value = fluxes[0], strips[1][0]
            if step < SUBSTEPS - 1:
                for strip, fe in zip(strips, fluxes):
                    f, cn, ce = strip
                    fn = cn * (turn(f, -6) - f)
                    strip[0] = f + fn - turn(fn, 6) + fe - turn(fe, 1)
            f = ext[step, here]
            nxt = ext[step + 1, here]
            fn_before = cn_ext[step : step + 1] * (nxt - f)
            for e in range(step + 1, rows + 5 - step):
                f = nxt
                nxt = ext[e + 1, here]
                at = 6 * (e - 1)
                fn = cn_ext[e : e + 1] * (nxt - f)
                f_east = jnp.where(lane == cols - 1, turn(east_value, cols - 1 - (at + 3)), turn(f, -1))
                fe = ce_ext[e : e + 1] * (f_east - f)
                fe_before = jnp.where(lane == 0, turn(west_flux, -(at + 2)), turn(fe, 1))
                ext[e, here] = f + fn - fn_before + fe - fe_before
                fn_before = fn

    wide = 256
    per = wide // cols
    for t in range(columns // wide):
        for j in range(per):
            r = t * per + j
            feeds[:, r * cols : (r + 1) * cols] = ext[r + 3].astype(BF16)

    tiles = columns // wide
    kind = iota((columns, wide), 0)

    @pl.loop(0, tiles)
    def _(t):
        at = pl.ds(pl.multiple_of(t * wide, wide), wide)
        pre = dot(w_in[...], feeds[:, at]) + w_land[...] * land[:, at]
        sig = 0.5 * jnp.tanh(0.5 * pre) + 0.5
        act = pre * sig
        a1 = act.astype(BF16)
        act1[:, at] = a1
        der1[:, at] = sig * (1.0 + pre - act)
        pre = dot(w_mid[...], a1)
        sig = 0.5 * jnp.tanh(0.5 * pre) + 0.5
        act = pre * sig
        a2 = act.astype(BF16)
        act2[:, at] = a2
        der2[:, at] = sig * (1.0 + pre - act)
        tend = dot(w_out[...], a2).astype(BF16).astype(F32)
        for j in range(per):
            ext[t * per + j + 3] += tend[:, j * cols : (j + 1) * cols]
        pick[:, at] = jnp.where(kind == place[:, at], 1.0, 0.0).astype(BF16)

    stores = [
        pltpu.make_async_copy(ext.at[r + 3], new_state.at[:, r, :], out_sem.at[r])
        for r in range(rows)
    ]
    for copy in stores:
        copy.start()

    part[...] = jnp.zeros_like(part)
    land_acc[...] = jnp.zeros_like(land_acc)

    @pl.loop(1, devs)
    def _(k):
        arrival(k).wait_recv()

    for j in range(columns // 128):
        cot_pl[:, j * 128 : (j + 1) * 128] = cot_rx[j * 128 : (j + 1) * 128].T

    hidden = w_in.shape[0]
    half = hidden // 2

    @pl.loop(0, tiles)
    def _(t):
        at = pl.ds(pl.multiple_of(t * wide, wide), wide)
        cg = dot(cot_pl[...], pick[:, at]).astype(BF16)
        out = dot_nt(cg, act2[:, at])
        part[4 * hidden - 2 * half : 4 * hidden - half] += out[:, :half]
        part[4 * hidden - half : 4 * hidden] += out[:, half:]
        b2 = (dot(wt_out[...], cg) * der2[:, at]).astype(BF16)
        mid = dot_nt(b2, act1[:, at])
        part[hidden : 2 * hidden] += mid[:, :half]
        part[2 * hidden : 3 * hidden] += mid[:, half:]
        b1f = dot(wt_mid[...], b2) * der1[:, at]
        b1 = b1f.astype(BF16)
        part[:hidden] += dot_nt(b1, feeds[:, at])
        weighed = b1.astype(F32) * land[:, at]
        gathered = weighed[:, :128]
        for j in range(1, wide // 128):
            gathered += weighed[:, j * 128 : (j + 1) * 128]
        land_acc[...] += gathered

    vec = jnp.sum(land_acc[...].T, axis=0, keepdims=True)
    sub_w = iota((PAD, half), 0)
    land_rows = jnp.where(sub_w == 0, vec[:, :half], jnp.where(sub_w == 1, vec[:, half:], 0.0))

    pairs = n_lat // 2
    core, chip = lax.rem(lat, 2), lat // 2
    levels = [
        (2, core, lambda p: (chip * 2 + p, lon), tx0, rx0, part, sum0, 0),
        (pairs, chip, lambda p: (p * 2 + core, lon), tx1, rx1, sum0, sum1, 1),
        (n_lon, lon, lambda p: (lat, p), tx2, rx2, sum1, None, 1 + pairs - 1),
    ]
    for size, mine, where, tx, rx, src, dst, base in levels:
        share = tx.shape[1] - PAD
        extra = land_rows.astype(BF16)
        for p in range(size):
            tx[p, :share] = src[p * share : (p + 1) * share].astype(BF16)
            tx[p, share:] = extra
        copies = []
        for k in range(1, size):
            there = lax.rem(mine + k, size)
            copies.append(
                pltpu.make_async_remote_copy(
                    src_ref=tx.at[there],
                    dst_ref=rx.at[size - 1 - k],
                    send_sem=red_send.at[base + k - 1],
                    recv_sem=red_recv.at[base + size - 1 - k],
                    device_id=where(there),
                    device_id_type=pl.DeviceIdType.MESH,
                )
            )
        for copy in copies:
            copy.start()
        for copy in copies:
            copy.wait()
        summed = tx[mine, :share].astype(F32)
        for s in range(size - 1):
            summed += rx[s, :share].astype(F32)
        land_rows = jnp.zeros((PAD, half), F32)
        for p in range(size):
            slot = lax.rem(p - mine - 1 + 2 * size, size)
            theirs = rx[jnp.minimum(slot, size - 2), share:].astype(F32)
            land_rows += jnp.where(p == mine, extra.astype(F32), theirs)
        if dst is not None:
            dst[...] = summed

    shares = [tx0.shape[1] - PAD, tx1.shape[1] - PAD, tx2.shape[1] - PAD]
    start0 = core * shares[0]
    start1 = start0 + chip * shares[1]
    start2 = start1 + lon * shares[2]
    grads[pl.ds(pl.multiple_of(start2, shares[2]), shares[2])] = summed.astype(BF16)
    grad_land[...] = land_rows
    spread = [
        (n_lon, lon, lambda p: (lat, p), start1, start2, shares[2], 0),
        (pairs, chip, lambda p: (p * 2 + core, lon), start0, start1, shares[1], n_lon - 1),
        (2, core, lambda p: (chip * 2 + p, lon), 0, start0, shares[0], n_lon + pairs - 2),
    ]
    for size, mine, where, group, start, share, base in spread:
        copies, waits = [], []
        for k in range(1, size):
            there = lax.rem(mine + k, size)
            piece = grads.at[pl.ds(pl.multiple_of(start, share), share)]
            landing = grads.at[pl.ds(pl.multiple_of(group + there * share, share), share)]
            copies.append(
                pltpu.make_async_remote_copy(
                    src_ref=piece,
                    dst_ref=piece,
                    send_sem=gat_send.at[base + k - 1],
                    recv_sem=gat_recv.at[base + size - 1 - k],
                    device_id=where(there),
                    device_id_type=pl.DeviceIdType.MESH,
                )
            )
            waits.append(
                pltpu.make_async_remote_copy(
                    src_ref=piece,
                    dst_ref=landing,
                    send_sem=gat_send.at[base + k - 1],
                    recv_sem=gat_recv.at[base + k - 1],
                    device_id=where(there),
                    device_id_type=pl.DeviceIdType.MESH,
                )
            )
        for copy in copies:
            copy.start()
        for copy in waits:
            copy.wait_recv()
        for copy in copies:
            copy.wait_send()

    @pl.loop(1, devs)
    def _(k):
        exchange(k).wait_send()

    for copy in stores:
        copy.wait()


def per_device(
    n_lat,
    n_lon,
    state,
    north_coef,
    east_coef,
    land_mask,
    owner_slot,
    w_in,
    w_mid,
    w_out,
    w_land,
    tend_cot,
):
    channels, rows, cols = state.shape
    hidden = w_in.shape[0]
    devs = n_lat * n_lon
    columns = rows * cols
    block = columns // devs
    row_index = lax.axis_index("lat") * rows + jnp.arange(rows, dtype=jnp.int32)
    north_face = jnp.where(row_index[:, None] < rows * n_lat - 1, north_coef, jnp.float32(0.0))
    slots = owner_slot.reshape(1, columns)
    place = slots // columns * block + slots % block
    land = land_mask.reshape(1, columns).astype(F32)
    total = 4 * hidden
    half = hidden // 2
    share0, share1, share2 = total // 2, total // n_lat, total // devs
    pairs = n_lat // 2
    tall = channels + PAD
    vmem = pl.BlockSpec(memory_space=pltpu.VMEM)
    anyspace = pl.BlockSpec(memory_space=pl.ANY)
    red = 1 + (pairs - 1) + (n_lon - 1)
    dma = pltpu.SemaphoreType.DMA
    new_state, grads, grad_land = pl.pallas_call(
        functools.partial(kernel, n_lat, n_lon),
        out_shape=(
            jax.ShapeDtypeStruct(state.shape, F32),
            jax.ShapeDtypeStruct((total, half), BF16),
            jax.ShapeDtypeStruct((PAD, half), F32),
        ),
        in_specs=[anyspace] + [vmem] * 9,
        out_specs=(anyspace, vmem, vmem),
        scratch_shapes=[
            pltpu.VMEM((rows + 6, channels, cols), F32),
            pltpu.VMEM((rows + 8, cols), F32),
            pltpu.VMEM((rows + 8, cols), F32),
            pltpu.VMEM((2, 3, tall, cols), BF16),
            pltpu.VMEM((tall, cols), BF16),
            pltpu.VMEM((2, 3, tall, cols), BF16),
            pltpu.VMEM((6, tall, cols), BF16),
            pltpu.VMEM((tall, cols), F32),
            pltpu.VMEM((tall, cols), F32),
            pltpu.VMEM((columns, channels), BF16),
            pltpu.VMEM((columns, channels), BF16),
            pltpu.VMEM((channels, columns), BF16),
            pltpu.VMEM((columns, columns), BF16),
            pltpu.VMEM((channels, columns), BF16),
            pltpu.VMEM((hidden, columns), BF16),
            pltpu.VMEM((hidden, columns), BF16),
            pltpu.VMEM((hidden, columns), F32),
            pltpu.VMEM((hidden, columns), F32),
            pltpu.VMEM((hidden, channels), BF16),
            pltpu.VMEM((hidden, hidden), BF16),
            pltpu.VMEM((total, half), F32),
            pltpu.VMEM((hidden, 128), F32),
            pltpu.VMEM((share0, half), F32),
            pltpu.VMEM((share1, half), F32),
            pltpu.VMEM((1, share0 + PAD, half), BF16),
            pltpu.VMEM((pairs - 1, share1 + PAD, half), BF16),
            pltpu.VMEM((n_lon - 1, share2 + PAD, half), BF16),
            pltpu.VMEM((2, share0 + PAD, half), BF16),
            pltpu.VMEM((pairs, share1 + PAD, half), BF16),
            pltpu.VMEM((n_lon, share2 + PAD, half), BF16),
            dma((rows,)),
            dma((rows,)),
            dma((8,)),
            dma((8,)),
            dma((devs,)),
            dma((devs,)),
            dma((red,)),
            dma((red,)),
            dma((red,)),
            dma((red,)),
        ],
        compiler_params=pltpu.CompilerParams(
            collective_id=0, has_side_effects=True, vmem_limit_bytes=56 * 1024 * 1024
        ),
    )(
        state,
        north_face,
        east_coef,
        land,
        place,
        w_in,
        w_mid,
        w_out,
        w_land.reshape(hidden, 1),
        tend_cot,
    )
    scale = jnp.float32((columns * devs) ** (-0.5))
    wide = grads.astype(F32) * scale
    grad_in = wide[:hidden]
    grad_mid = jnp.concatenate([wide[hidden : 2 * hidden], wide[2 * hidden : 3 * hidden]], 1)
    grad_out = jnp.concatenate([wide[3 * hidden : 3 * hidden + half], wide[3 * hidden + half :]], 1)
    return new_state, grad_in, grad_mid, grad_out, grad_land[:2].reshape(hidden) * scale


def solution(mesh):
    n_lat, n_lon = mesh.shape["lat"], mesh.shape["lon"]
    placed = (
        P(None, "lat", "lon"),
        P("lat", "lon"),
        P("lat", "lon"),
        P("lat", "lon"),
        P("lat", "lon"),
        P(),
        P(),
        P(),
        P(),
        P(None, ("lat", "lon")),
    )
    return jax.shard_map(
        functools.partial(per_device, n_lat, n_lon),
        mesh=mesh,
        in_specs=placed,
        out_specs=(P(None, "lat", "lon"), P(), P(), P(), P()),
        check_vma=False,
    )
```
